128 devices in a mesh: cp: 32 (over z, y, core), tp: 4 (over x).
Axes of the slice: x: 4, y: 4, z: 4, core: 2. Of those that a mesh axis runs over, the one named last changes fastest.
Arguments:
- queries: bfloat16 [24576, 64, 128], P('cp', 'tp'), may hold values from -9 to 9
- key_states: bfloat16 [24576, 8, 128], P(('cp', 'tp')), may hold values from -4.5 to 4.5
- value_states: bfloat16 [24576, 8, 128], P(('cp', 'tp')), may hold values from -6 to 6
- doc_ids: int32 [24576], P('cp'), may hold values from 0 to 31, never falling along the last dimension, each value on 1 to 2305 neighbouring positions
Outputs:
- attended: bfloat16 [24576, 64, 128], P('cp', 'tp')
The draws below stay inside these ranges and needn't reach their ends.
Inputs may be any that keep to these rules, and one draw needn't show every extreme that they name: doc_ids never fall along the sequence; each document holds 1 to 2305 tokens, and one holds exactly 2305.
All inputs are finite; a program needn't handle non-finite values.
Results may differ from the reference program's by a relative error of at most 0.0055.
Values may be sent and summed in bfloat16 or wider, within the bound.
No kernel may reach another device: no remote copies, remote signals or barrier semaphores. Data moves between devices by JAX's collectives and lax.ppermute only.
A program may use at most 320 MiB of HBM per device.

```python
import math
import jax
import jax.numpy as jnp
import numpy as np
from jax import lax

HQ = 64
HK = 8
DH = 128
S_DEV = 768
WIN = 4
TOKENS = 24576
DOCS = 32
MOST = 2305
N_CP = 32


def draw_key_states(key, part):
    key = jax.random.fold_in(key, 3)
    keys = jnp.clip(jax.random.normal(key, (TOKENS, HK, DH), jnp.float32), -4.5, 4.5)
    return keys.astype(jnp.bfloat16)


def draw_queries(key, part):
    key = jax.random.fold_in(key, 5)
    base = jnp.clip(jax.random.normal(key, (TOKENS, HQ, DH), jnp.float32), -4.5, 4.5)
    return base.astype(jnp.bfloat16)


def level_of(rng, extent, cuts, least, high):
    loudness, own = 1.0, jax.random.fold_in(rng, 6)
    for axis_at, blocks in cuts:
        steps = jnp.exp(jax.random.uniform(jax.random.fold_in(own, axis_at), (blocks,), jnp.float32, least / len(cuts), high / len(cuts)))
        loudness = loudness * jnp.repeat(steps, extent[axis_at] // blocks).reshape([-1 if axis == axis_at else 1 for axis in range(len(extent))])
    return loudness


def profile(amount, total, most, lean):
    loads = [(1 << 20) // math.isqrt(standing ** lean) + 1 for standing in range(2, amount + 1)]
    surplus, counts = total - most - (amount - 1), [1] * (amount - 1)
    while surplus > 0:
        movable = [i for i in range(amount - 1) if counts[i] < most]
        mass, budget = sum([loads[i] for i in movable]), surplus
        for i in movable:
            more = min(most - counts[i], max(1, budget * loads[i] // mass), surplus)
            counts[i] = counts[i] + more
            surplus = surplus - more
    return np.array([most] + counts)


def ragged(own_key, amount, total, bound, slope):
    if amount == 2:
        one = jax.random.randint(own_key, (), max(1, total - bound), min(bound, total - 1) + 1)
        return jnp.stack([one, total - one])
    lengths = jnp.asarray(profile(amount, total, bound, slope), jnp.int32)
    twos = (amount - 1) // 2
    giver, receiver = lengths[1:1 + 2 * twos:2], lengths[2:2 + 2 * twos:2]
    slack = jnp.minimum(giver - 1, bound - receiver)
    passed = jax.random.randint(jax.random.fold_in(own_key, 1), (twos,), 0, 1 << 20) % (slack + 1)
    lengths = lengths.at[1:1 + 2 * twos:2].set(giver - passed).at[2:2 + 2 * twos:2].set(receiver + passed)
    return lengths[jax.random.permutation(jax.random.fold_in(own_key, 2), amount)]


def noise(own_key, extent, deviation, most, shards=(), kind=jnp.bfloat16):
    loudness = level_of(own_key, extent, shards, -0.22, 0.18) if shards else 1.0
    array = jax.random.normal(own_key, extent, jnp.float32) * deviation * loudness
    return jnp.minimum(jnp.maximum(array, -most), most).astype(kind)


def setup_inputs(seed: int = 0) -> dict:
    streams_of = jax.random.split(jax.random.key(seed), 5)
    queries = draw_queries(jax.random.fold_in(streams_of[4], 71), 0)
    key_states = draw_key_states(jax.random.fold_in(streams_of[4], 71), 0)
    value_states = noise(streams_of[2], (TOKENS, HK, DH), 1.0, 6.0, ((0, 128),))
    doc_ids = jnp.searchsorted(jnp.cumsum(ragged(streams_of[3], DOCS, TOKENS, MOST, 2)), jnp.arange(TOKENS), side="right").astype(jnp.int32)
    return dict(queries=queries, key_states=key_states, value_states=value_states, doc_ids=doc_ids)


def reference(queries, key_states, value_states, doc_ids):
    group = HQ // HK
    scale = 1.0 / math.sqrt(DH)
    pad = (WIN - 1) * S_DEV
    keys_pad = jnp.concatenate([jnp.zeros((pad, HK, DH), jnp.bfloat16), key_states], axis=0)
    vals_pad = jnp.concatenate([jnp.zeros((pad, HK, DH), jnp.bfloat16), value_states], axis=0)
    tags_pad = jnp.concatenate([jnp.full((pad,), -1, jnp.int32), doc_ids.astype(jnp.int32)], axis=0)

    def one_block(block):
        start = (block * S_DEV).astype(jnp.int32)
        q_blk = lax.dynamic_slice_in_dim(queries, start, S_DEV, 0).astype(jnp.float32).reshape(S_DEV, HK, group, DH)
        k_blk = lax.dynamic_slice_in_dim(keys_pad, start, WIN * S_DEV, 0).astype(jnp.float32)
        v_blk = lax.dynamic_slice_in_dim(vals_pad, start, WIN * S_DEV, 0).astype(jnp.float32)
        q_tag = lax.dynamic_slice_in_dim(doc_ids.astype(jnp.int32), start, S_DEV, 0)
        k_tag = lax.dynamic_slice_in_dim(tags_pad, start, WIN * S_DEV, 0)
        q_pos = jnp.arange(S_DEV, dtype=jnp.int32) + pad
        k_pos = jnp.arange(WIN * S_DEV, dtype=jnp.int32)
        allowed = (q_tag[:, None] == k_tag[None, :]) & (k_pos[None, :] <= q_pos[:, None])
        scores = jnp.einsum('sngd,tnd->ngst', q_blk, k_blk) * scale
        scores = jnp.where(allowed[None, None], scores, -1e+30)
        top = lax.optimization_barrier(jnp.max(scores, axis=-1, keepdims=True))
        weights = jnp.where(allowed[None, None], jnp.exp(scores - top), 0.0)
        total = lax.optimization_barrier(jnp.sum(weights, axis=-1))
        rounded = lax.optimization_barrier(weights.astype(jnp.bfloat16)).astype(jnp.float32)
        out = jnp.einsum('ngst,tnd->ngsd', rounded, v_blk) / total[..., None]
        return out.transpose(2, 0, 1, 3).reshape(S_DEV, HQ, DH).astype(jnp.bfloat16)
    blocks = lax.map(one_block, jnp.arange(N_CP, dtype=jnp.int32))
    return blocks.reshape(TOKENS, HQ, DH)
```

```python
import functools
import math

import jax
import jax.numpy as jnp
from jax import lax
from jax.experimental import pallas as pl
from jax.experimental.pallas import tpu as pltpu
from jax.sharding import PartitionSpec as P

WIN = 4
NT = (((1,), (1,)), ((), ()))
LOG2E = 1.4426950408889634
SAFE = 100.0
NEG = -1e30
TILE = 128
ROWS = 144
VMEM_LIMIT = 48 * 2**20


def top_norm(x):
    xf = x.astype(jnp.float32)
    return jnp.max(jnp.sum(xf * xf, axis=-1, keepdims=True))


def safe(q_norm, k_norm):
    return q_norm * k_norm <= SAFE * abs(SAFE)


def local_kernel(group, q_ref, kv_ref, low_ref, qs_ref, acc_ref, norm_ref, vt_ref, kn_ref):
    step = pl.program_id(0)
    rows, width = kv_ref.shape[0], q_ref.shape[2]
    kv_heads = q_ref.shape[1] // group
    lanes = TILE * group
    scale = LOG2E / math.sqrt(width)

    @pl.when(step == 0)
    def _():
        kn = jnp.float32(0.0)
        for g in range(kv_heads):
            base = 2 * width * g
            kn = jnp.maximum(kn, top_norm(kv_ref[:, base : base + width]))
            vt_ref[g, :width] = kv_ref[:, base + width : base + 2 * width].T
            vt_ref[g, width:] = jnp.ones((ROWS - width, rows), jnp.bfloat16)
        kn_ref[0] = kn

    qf = q_ref[...].astype(jnp.float32) * scale
    for g in range(kv_heads):
        qs_ref[g] = qf[:, group * g : group * (g + 1)].reshape(lanes, width).astype(jnp.bfloat16)
    qn = jnp.maximum(top_norm(qs_ref[0]), top_norm(qs_ref[1]))
    norm_ref[step] = qn
    fast = safe(qn, kn_ref[0])
    low = low_ref[0:1]
    token = step * TILE + lax.broadcasted_iota(jnp.int32, (1, lanes), 1) // group

    for i in range(rows // TILE):
        keys = (i + 1) * TILE

        def parts(g):
            k = kv_ref[:keys, 2 * width * g : 2 * width * g + width]
            s = lax.dot_general(k, qs_ref[g], NT, preferred_element_type=jnp.float32)
            at = lax.broadcasted_iota(jnp.int32, (keys, lanes), 0)
            return s, (at >= low) & (at <= token)

        @pl.when((step == i) & fast)
        def _():
            for g in range(kv_heads):
                s, ok = parts(g)
                p = jnp.where(ok, jnp.exp2(s), 0.0).astype(jnp.bfloat16)
                out = jnp.dot(vt_ref[g, :, :keys], p, preferred_element_type=jnp.float32)
                acc_ref[g, : width + 8] = out[: width + 8]
                acc_ref[g, width + 8 :] = jnp.zeros((ROWS - width - 8, lanes), jnp.float32)

        @pl.when((step == i) & jnp.logical_not(fast))
        def _():
            for g in range(kv_heads):
                s, ok = parts(g)
                m = jnp.max(jnp.where(ok, s, NEG), axis=0, keepdims=True)
                p = jnp.where(ok, jnp.exp2(s - m), 0.0).astype(jnp.bfloat16)
                out = jnp.dot(vt_ref[g, :, :keys], p, preferred_element_type=jnp.float32)
                acc_ref[g, : width + 8] = out[: width + 8]
                acc_ref[g, width + 8 :] = jnp.broadcast_to(m, (ROWS - width - 8, lanes))


def far_kernel(group, blocks, count_ref, norm_in_ref, qs_ref, acc_in_ref, *refs):
    kv_refs, (o_ref, acc_ref, vt_ref, kn_ref) = refs[:blocks], refs[blocks:]
    step = pl.program_id(0)
    kv_heads, lanes, width = qs_ref.shape
    rows = kv_refs[0].shape[0]
    small = 256

    @pl.when(step == 0)
    def _():
        for b in range(blocks):
            kn_ref[b] = 0.0

            @pl.when(count_ref[b] > 0)
            def _():
                kn = jnp.float32(0.0)
                valid = lax.broadcasted_iota(jnp.int32, (1, rows), 1) >= rows - count_ref[b]
                for g in range(kv_heads):
                    base = 2 * width * g
                    kn = jnp.maximum(kn, top_norm(kv_refs[b][:, base : base + width]))
                    vt = kv_refs[b][:, base + width : base + 2 * width].astype(jnp.float32).T
                    vt_ref[b, g, :width] = jnp.where(valid, vt, 0.0).astype(jnp.bfloat16)
                    ones = jnp.ones((ROWS - width, rows), jnp.float32)
                    vt_ref[b, g, width:] = jnp.where(valid, ones, 0.0).astype(jnp.bfloat16)
                kn_ref[b] = kn

    acc_ref[...] = acc_in_ref[...]
    reach = count_ref[blocks]
    qn = norm_in_ref[step]
    kn = kn_ref[0]
    for b in range(1, blocks):
        kn = jnp.maximum(kn, kn_ref[b])
    fast = safe(qn, kn) & (jnp.max(jnp.abs(acc_in_ref[0, width + 8 :])) == 0.0)
    fast = fast & (jnp.max(jnp.abs(acc_in_ref[1, width + 8 :])) == 0.0)
    token = step * TILE + lax.broadcasted_iota(jnp.int32, (1, lanes), 1) // group
    mine = token < reach
    some = step * TILE < reach

    for b in range(blocks):
        count = count_ref[b]

        def quick(start):
            for g in range(kv_heads):
                k = kv_refs[b][start:, 2 * width * g : 2 * width * g + width]
                s = lax.dot_general(k, qs_ref[g], NT, preferred_element_type=jnp.float32)
                p = jnp.exp2(s).astype(jnp.bfloat16)
                out = jnp.dot(vt_ref[b, g, :, start:], p, preferred_element_type=jnp.float32)
                acc_ref[g, : width + 8] += jnp.where(mine, out[: width + 8], 0.0)

        @pl.when(some & fast & (count > small))
        def _():
            quick(0)

        @pl.when(some & fast & (count > 0) & (count <= small))
        def _():
            quick(rows - small)

        @pl.when(some & (count > 0) & jnp.logical_not(fast))
        def _():
            def general(j, carry):
                first = pl.multiple_of(j * small, small)
                for g in range(kv_heads):
                    k = kv_refs[b][pl.ds(first, small), 2 * width * g : 2 * width * g + width]
                    s = lax.dot_general(k, qs_ref[g], NT, preferred_element_type=jnp.float32)
                    at = first + lax.broadcasted_iota(jnp.int32, (small, lanes), 0)
                    ok = (at >= rows - count) & mine
                    old = acc_ref[g, width + 8 : width + 9]
                    m = jnp.maximum(old, jnp.max(jnp.where(ok, s, NEG), axis=0, keepdims=True))
                    p = jnp.where(ok, jnp.exp2(s - m), 0.0).astype(jnp.bfloat16)
                    vt = vt_ref[b, g, :, pl.ds(first, small)]
                    out = jnp.dot(vt, p, preferred_element_type=jnp.float32)
                    factor = jnp.exp2(old - m)
                    acc_ref[g, : width + 8] = acc_ref[g, : width + 8] * factor + out[: width + 8]
                    acc_ref[g, width + 8 :] = jnp.broadcast_to(m, (ROWS - width - 8, lanes))
                return carry

            lax.fori_loop(0, rows // small, general, 0)

    outs = []
    for g in range(kv_heads):
        o = acc_ref[g, :width] * (1.0 / acc_ref[g, width : width + 1])
        outs.append(o.T.reshape(TILE, group, width))
    o_ref[...] = jnp.concatenate(outs, axis=1).astype(jnp.bfloat16)


def shards(queries, key_states, value_states, doc_ids):
    rows, q_heads, width = queries.shape
    tp = lax.axis_size("tp")
    cp = lax.axis_size("cp")
    part = key_states.shape[0]
    kv_heads = key_states.shape[1] // tp
    group = q_heads // kv_heads
    lanes = TILE * group
    steps = rows // TILE

    tag = doc_ids + 1
    reach = jnp.sum((tag == tag[0]).astype(jnp.int32))
    back = jnp.int32(0)
    for d in range(1, WIN):
        far = lax.ppermute(tag, "cp", [(i, i + d) for i in range(cp - d)])
        back = back + jnp.sum((far == tag[0]).astype(jnp.int32))
    low = jnp.sum((tag[None, :] < tag[:, None]).astype(jnp.int32), axis=1)
    low = jnp.broadcast_to(jnp.repeat(low, group)[None], (8, rows * group))

    pack = lambda x: x.reshape(part, tp, kv_heads, 1, width)
    kv = jnp.concatenate([pack(key_states), pack(value_states)], axis=3)
    kv = kv.reshape(part, tp, 2 * kv_heads * width).transpose(1, 0, 2)
    kv = lax.all_to_all(kv, "tp", split_axis=0, concat_axis=0, tiled=True)
    kv = kv.reshape(rows, 2 * kv_heads * width)

    flip = [(i, i ^ 1) for i in range(cp)]
    two = lax.ppermute(kv, "cp", [(i, i + 2) for i in range(cp - 2)])
    own_flip = lax.ppermute(kv, "cp", flip)
    three = lax.ppermute(kv, "cp", [(i, i + 3) for i in range(1, cp - 3, 2)])
    two_flip = lax.ppermute(two, "cp", flip)

    params = pltpu.CompilerParams(vmem_limit_bytes=VMEM_LIMIT)
    whole = pl.BlockSpec((rows, 2 * kv_heads * width), lambda i: (0, 0))
    qs_spec = pl.BlockSpec((kv_heads, lanes, width), lambda i: (0, i, 0))
    acc_spec = pl.BlockSpec((kv_heads, ROWS, lanes), lambda i: (0, 0, i))
    q_spec = pl.BlockSpec((TILE, q_heads, width), lambda i: (i, 0, 0))
    smem = pl.BlockSpec(memory_space=pltpu.SMEM)
    qs, acc, norms = pl.pallas_call(
        functools.partial(local_kernel, group),
        grid=(steps,),
        in_specs=[q_spec, whole, pl.BlockSpec((8, lanes), lambda i: (0, i))],
        out_specs=[qs_spec, acc_spec, smem],
        out_shape=[
            jax.ShapeDtypeStruct((kv_heads, rows * group, width), jnp.bfloat16),
            jax.ShapeDtypeStruct((kv_heads, ROWS, rows * group), jnp.float32),
            jax.ShapeDtypeStruct((steps,), jnp.float32),
        ],
        scratch_shapes=[
            pltpu.VMEM((kv_heads, ROWS, rows), jnp.bfloat16),
            pltpu.SMEM((1,), jnp.float32),
        ],
        compiler_params=params,
        cost_estimate=pl.CostEstimate(flops=8 * 10**9, bytes_accessed=2 * 10**7, transcendentals=0),
        name="local",
    )(queries, kv, low)

    odd = lax.axis_index("cp") % 2 == 1
    behind = lambda d: jnp.clip(back - rows * (d - 1), 0, rows)
    counts = jnp.stack(
        [
            jnp.where(odd, behind(1), 0),
            behind(2),
            jnp.where(odd, behind(3), behind(1)),
            jnp.where(odd, 0, behind(3)),
            reach,
        ]
    ).astype(jnp.int32)
    blocks = 4
    return pl.pallas_call(
        functools.partial(far_kernel, group, blocks),
        grid=(steps,),
        in_specs=[smem, smem, qs_spec, acc_spec] + [whole] * blocks,
        out_specs=q_spec,
        out_shape=jax.ShapeDtypeStruct(queries.shape, jnp.bfloat16),
        scratch_shapes=[
            pltpu.VMEM((kv_heads, ROWS, lanes), jnp.float32),
            pltpu.VMEM((blocks, kv_heads, ROWS, rows), jnp.bfloat16),
            pltpu.SMEM((blocks,), jnp.float32),
        ],
        compiler_params=params,
        cost_estimate=pl.CostEstimate(flops=2 * 10**10, bytes_accessed=2 * 10**7, transcendentals=0),
        name="far",
    )(counts, norms, qs, acc, own_flip, two, two_flip, three)


def solution(mesh):
    in_specs = (
        P("cp", "tp", None),
        P(("cp", "tp"), None, None),
        P(("cp", "tp"), None, None),
        P("cp"),
    )
    out_specs = P("cp", "tp", None)
    return jax.shard_map(shards, mesh=mesh, in_specs=in_specs, out_specs=out_specs, check_vma=False)
```

```python
import functools
import math

import jax
import jax.numpy as jnp
from jax import lax
from jax.experimental import pallas as pl
from jax.experimental.pallas import tpu as pltpu
from jax.sharding import PartitionSpec as P

WIN = 4
NT = (((1,), (1,)), ((), ()))
LOG2E = 1.4426950408889634
SAFE = 100.0
NEG = -1e30
TILE = 256
SMALL = 256
PAD = 16
VMEM_LIMIT = 48 * 2**20


def top_norm(x):
    xf = x.astype(jnp.float32)
    return jnp.max(jnp.sum(xf * xf, axis=-1, keepdims=True))


def pack_kernel(tp, kv_heads, k_ref, v_ref, *refs):
    out_refs, buf = refs[:-1], refs[-1]
    part, width = buf.shape[1], k_ref.shape[1]
    heads = k_ref.shape[0] // part
    n = 16 * heads
    row = lax.broadcasted_iota(jnp.int32, (n, n), 0)
    col = lax.broadcasted_iota(jnp.int32, (n, n), 1)
    swap = (col == (row % 16) * heads + row // 16).astype(jnp.bfloat16)
    for which, ref in enumerate((k_ref, v_ref)):
        for c in range(part // 16):
            y = jnp.dot(swap, ref[c * n : (c + 1) * n], preferred_element_type=jnp.float32)
            y = y.astype(jnp.bfloat16)
            for h in range(heads):
                at = (2 * (h % kv_heads) + which) * width
                buf[h // kv_heads, c * 16 : c * 16 + 16, at : at + width] = y[16 * h : 16 * h + 16]
    me = lax.axis_index("tp")
    for d in range(tp):
        out_refs[d][...] = buf[lax.rem(me + d, tp)]


def scale_kernel(group, low_ref, q_ref, qs_ref, norm_ref):
    step = pl.program_id(0)
    tokens, heads, width = q_ref.shape
    qf = q_ref[...].astype(jnp.float32) * (LOG2E / math.sqrt(width))
    top = jnp.float32(0.0)
    for g in range(heads // group):
        x = qf[:, group * g : group * (g + 1)].reshape(tokens * group, width)
        qs_ref[g] = x.astype(jnp.bfloat16)
        top = jnp.maximum(top, top_norm(x))
    norm_ref[step] = top * 1.02


def assemble_kernel(tp, kv_heads, norm_ref, tag_ref, *refs):
    parts, o_ref, v_ref = refs[:tp], refs[tp], refs[tp + 1]
    part, width = parts[0].shape[0], v_ref.shape[1]
    rows = part * tp
    me = lax.axis_index("tp")
    for g in range(kv_heads):
        for d in range(tp):
            at = pl.multiple_of(lax.rem(me + tp - d, tp) * part, 16)
            o_ref[g, pl.ds(at, part)] = parts[d][:, 2 * width * g : 2 * width * g + width]
            v_ref[pl.ds(at, part)] = parts[d][:, 2 * width * g + width : 2 * width * (g + 1)].astype(jnp.float32)
        for j in range(rows // width):
            block = v_ref[j * width : (j + 1) * width].T
            o_ref[g, rows + j * width : rows + (j + 1) * width] = block.astype(jnp.bfloat16)
        o_ref[g, 2 * rows : 2 * rows + PAD] = tag_ref[...]
        top = top_norm(o_ref[g, :rows]) * 1.02
        o_ref[g, 2 * rows + PAD :] = jnp.full((PAD, width), top, jnp.float32).astype(jnp.bfloat16)


def fill_values(vt_ref, at, kv_ref, g, rows, count):
    width = kv_ref.shape[-1]
    more = vt_ref.shape[-2] - width
    for j in range(rows // width):
        cols = slice(j * width, (j + 1) * width)
        valid = j * width + lax.broadcasted_iota(jnp.int32, (1, width), 1) >= rows - count
        vt = kv_ref[g, rows + j * width : rows + (j + 1) * width].astype(jnp.float32)
        vt_ref[(*at, slice(0, width), cols)] = jnp.where(valid, vt, 0.0).astype(jnp.bfloat16)
        ones = jnp.ones((more, width), jnp.float32)
        vt_ref[(*at, slice(width, width + more), cols)] = jnp.where(valid, ones, 0.0).astype(jnp.bfloat16)


def general_tile(acc_ref, g, s, ok, vt):
    sums = vt.shape[0]
    old = acc_ref[g, sums : sums + 1]
    m = jnp.maximum(old, jnp.max(jnp.where(ok, s, NEG), axis=0, keepdims=True))
    p = jnp.where(ok, jnp.exp2(s - m), 0.0).astype(jnp.bfloat16)
    o = jnp.dot(vt, p, preferred_element_type=jnp.float32)
    acc_ref[g, :sums] = acc_ref[g, :sums] * jnp.exp2(old - m) + o
    acc_ref[g, sums:] = jnp.broadcast_to(m, (8, s.shape[1]))


def local_kernel(group, norm_ref, low_ref, qs_ref, own_ref, acc_ref, vt_ref):
    step = pl.program_id(1)
    width = own_ref.shape[2]
    rows = vt_ref.shape[1]
    sums = vt_ref.shape[0]
    lanes = TILE * group

    @pl.when(step == 0)
    def _():
        fill_values(vt_ref, (), own_ref, 0, rows, rows)

    kn = jnp.max(own_ref[0, 2 * rows + PAD :].astype(jnp.float32))
    fast = norm_ref[step] * kn <= SAFE * abs(SAFE)
    token = step * TILE + lax.broadcasted_iota(jnp.int32, (1, lanes), 1) // group
    low = low_ref[0:1]

    for i in range(rows // TILE):

        @pl.when(fast & (step == i))
        def _():
            keys = (i + 1) * TILE
            s = lax.dot_general(own_ref[0, :keys], qs_ref[0], NT, preferred_element_type=jnp.float32)
            at = lax.broadcasted_iota(jnp.int32, (keys, lanes), 0)
            p = jnp.where((at >= low) & (at <= token), jnp.exp2(s), 0.0).astype(jnp.bfloat16)
            acc_ref[0, :sums] = jnp.dot(vt_ref[:, :keys], p, preferred_element_type=jnp.float32)
            acc_ref[0, sums:] = jnp.zeros((8, lanes), jnp.float32)

    @pl.when(jnp.logical_not(fast))
    def _():
        acc_ref[0, :sums] = jnp.zeros((sums, lanes), jnp.float32)
        acc_ref[0, sums:] = jnp.full((8, lanes), NEG, jnp.float32)

        def tile(j, carry):
            at = pl.multiple_of(j * SMALL, SMALL)
            s = lax.dot_general(own_ref[0, pl.ds(at, SMALL)], qs_ref[0], NT, preferred_element_type=jnp.float32)
            pos = at + lax.broadcasted_iota(jnp.int32, (SMALL, lanes), 0)
            general_tile(acc_ref, 0, s, (pos >= low) & (pos <= token), vt_ref[:, pl.ds(at, SMALL)])
            return carry

        lax.fori_loop(0, ((step + 1) * TILE + SMALL - 1) // SMALL, tile, 0)


def far_kernel(
    group, norm_ref, tag_ref, qs_ref, acc_in_ref, flip_ref, two_ref, two_flip_ref, three_ref,
    o_ref, k_ref, vt_ref, acc_ref, n_ref, kn_ref
):
    step = pl.program_id(0)
    kv_heads, lanes, width = qs_ref.shape
    rows = vt_ref.shape[-1]
    sums = vt_ref.shape[-2]
    home = (WIN - 1) * rows

    @pl.when(step == 0)
    def _():
        odd = lax.rem(lax.axis_index("cp"), 2) == 1
        even = jnp.logical_not(odd)
        own = tag_ref[...].astype(jnp.float32)
        at = lax.broadcasted_iota(jnp.int32, own.shape, 0) * width
        at = at + lax.broadcasted_iota(jnp.int32, own.shape, 1)
        first = jnp.max(jnp.where(at == 0, own, 0.0))
        count = lambda x: jnp.sum((x.astype(jnp.float32) == first).astype(jnp.float32)).astype(jnp.int32)
        same = lambda ref: count(ref[0, 2 * rows : 2 * rows + PAD])
        n_ref[0] = count(own)
        n_ref[1] = jnp.where(odd, same(flip_ref), same(two_flip_ref))
        n_ref[2] = same(two_ref)
        n_ref[3] = jnp.where(odd, same(two_flip_ref), same(three_ref))
        kn_ref[0] = 0.0
        for slot, d, ref, when in (
            (2, 1, flip_ref, odd),
            (2, 1, two_flip_ref, even),
            (1, 2, two_ref, odd | even),
            (0, 3, two_flip_ref, odd),
            (0, 3, three_ref, even),
        ):

            @pl.when(when & (n_ref[d] > 0))
            def _():
                for g in range(kv_heads):
                    k_ref[g, slot * rows : (slot + 1) * rows] = ref[g, :rows]
                    fill_values(vt_ref, (g, slot), ref, g, rows, n_ref[d])
                    kn_ref[0] = jnp.maximum(kn_ref[0], jnp.max(ref[g, 2 * rows + PAD :].astype(jnp.float32)))

    acc_ref[...] = acc_in_ref[...]
    reach = n_ref[0]
    back = n_ref[1] + n_ref[2] + n_ref[3]
    fast = norm_ref[step] * kn_ref[0] <= SAFE * abs(SAFE)
    for g in range(kv_heads):
        fast = fast & (jnp.max(jnp.abs(acc_in_ref[g, sums:])) == 0.0)
    token = step * TILE + lax.broadcasted_iota(jnp.int32, (1, lanes), 1) // group
    mine = token < reach
    some = step * TILE < reach

    def scores(g, at, keys):
        return lax.dot_general(k_ref[g, pl.ds(at, keys)], qs_ref[g], NT, preferred_element_type=jnp.float32)

    @pl.when(fast & some & (back > 0))
    def _():
        first = jnp.where(back > rows, 1, 2)

        def block(j, carry):
            g = lax.rem(j, kv_heads)
            slot = first + j // kv_heads
            p = jnp.exp2(scores(g, pl.multiple_of(slot * rows, rows), rows)).astype(jnp.bfloat16)
            o = jnp.dot(vt_ref[g, slot], p, preferred_element_type=jnp.float32)
            acc_ref[g, :sums] += jnp.where(mine, o, 0.0)
            return carry

        lax.fori_loop(0, (WIN - 1 - first) * kv_heads, block, 0)

    @pl.when(fast & some & (back > 2 * rows))
    def _():
        def tile(j, carry):
            g = lax.rem(j, kv_heads)
            at = pl.multiple_of(j // kv_heads * SMALL, SMALL)
            p = jnp.exp2(scores(g, at, SMALL)).astype(jnp.bfloat16)
            o = jnp.dot(vt_ref[g, 0, :, pl.ds(at, SMALL)], p, preferred_element_type=jnp.float32)
            acc_ref[g, :sums] += jnp.where(mine, o, 0.0)
            return carry

        lax.fori_loop((home - back) // SMALL * kv_heads, rows // SMALL * kv_heads, tile, 0)

    @pl.when(jnp.logical_not(fast) & some)
    def _():
        def tile(j, carry):
            g = lax.rem(j, kv_heads)
            at = pl.multiple_of(j // kv_heads * SMALL, SMALL)
            s = scores(g, at, SMALL)
            pos = at + lax.broadcasted_iota(jnp.int32, (SMALL, lanes), 0)
            slot = at // rows
            vt = vt_ref[g, slot, :, pl.ds(pl.multiple_of(at - slot * rows, SMALL), SMALL)]
            general_tile(acc_ref, g, s, (pos >= home - back) & mine, vt)
            return carry

        lax.fori_loop((home - back) // SMALL * kv_heads, home // SMALL * kv_heads, tile, 0)

    outs = []
    for g in range(kv_heads):
        o = acc_ref[g, :width] * (1.0 / acc_ref[g, width : width + 1])
        outs.append(o.T.reshape(TILE, group, width))
    o_ref[...] = jnp.concatenate(outs, axis=1).astype(jnp.bfloat16)


def shards(queries, key_states, value_states, doc_ids):
    rows, q_heads, width = queries.shape
    tp = lax.axis_size("tp")
    cp = lax.axis_size("cp")
    part, heads = key_states.shape[:2]
    kv_heads = heads // tp
    group = q_heads // kv_heads
    lanes = TILE * group
    steps = rows // TILE
    params = pltpu.CompilerParams(vmem_limit_bytes=VMEM_LIMIT)
    vmem = pl.BlockSpec(memory_space=pltpu.VMEM)
    smem = pl.BlockSpec(memory_space=pltpu.SMEM)

    tag = (doc_ids + 1).astype(jnp.bfloat16).reshape(rows // width, width)
    tag = jnp.pad(tag, ((0, PAD - tag.shape[0]), (0, 0)))
    low = jnp.sum((doc_ids[None, :] < doc_ids[:, None]).astype(jnp.int32), axis=1)
    low = jnp.broadcast_to(jnp.repeat(low, group)[None], (8, rows * group))

    pieces = pl.pallas_call(
        functools.partial(pack_kernel, tp, kv_heads),
        in_specs=[vmem, vmem],
        out_specs=[vmem] * tp,
        out_shape=[jax.ShapeDtypeStruct((part, 2 * kv_heads * width), jnp.bfloat16)] * tp,
        scratch_shapes=[pltpu.VMEM((tp, part, 2 * kv_heads * width), jnp.bfloat16)],
        compiler_params=params,
        name="pack",
    )(key_states.reshape(part * heads, width), value_states.reshape(part * heads, width))
    mine = [pieces[0]]
    for d in range(1, tp):
        mine.append(lax.ppermute(pieces[d], "tp", [(i, (i + d) % tp) for i in range(tp)]))

    qs, norms = pl.pallas_call(
        functools.partial(scale_kernel, group),
        grid=(steps,),
        in_specs=[pl.BlockSpec(memory_space=pl.ANY), pl.BlockSpec((TILE, q_heads, width), lambda i: (i, 0, 0))],
        out_specs=[pl.BlockSpec((kv_heads, lanes, width), lambda i: (0, i, 0)), smem],
        out_shape=[
            jax.ShapeDtypeStruct((kv_heads, rows * group, width), jnp.bfloat16),
            jax.ShapeDtypeStruct((steps,), jnp.float32),
        ],
        compiler_params=params,
        name="scale",
    )(low, queries)
    size = (kv_heads, 2 * rows + 2 * PAD, width)
    own = pl.pallas_call(
        functools.partial(assemble_kernel, tp, kv_heads),
        in_specs=[smem] + [vmem] * (tp + 1),
        out_specs=vmem,
        out_shape=jax.ShapeDtypeStruct(size, jnp.bfloat16),
        scratch_shapes=[pltpu.VMEM((rows, width), jnp.float32)],
        compiler_params=params,
        name="assemble",
    )(norms, tag, *mine)

    flip_route = [(i, i ^ 1) for i in range(cp)]
    two = lax.ppermute(own, "cp", [(i, i + 2) for i in range(cp - 2)])
    flip = lax.ppermute(own, "cp", flip_route)

    sums = width + 16
    acc = pl.pallas_call(
        functools.partial(local_kernel, group),
        grid=(kv_heads, steps),
        in_specs=[
            smem,
            pl.BlockSpec((8, lanes), lambda g, i: (0, i)),
            pl.BlockSpec((1, lanes, width), lambda g, i: (g, i, 0)),
            pl.BlockSpec((1, *size[1:]), lambda g, i: (g, 0, 0)),
        ],
        out_specs=pl.BlockSpec((1, sums + 8, lanes), lambda g, i: (g, 0, i)),
        out_shape=jax.ShapeDtypeStruct((kv_heads, sums + 8, rows * group), jnp.float32),
        scratch_shapes=[pltpu.VMEM((sums, rows), jnp.bfloat16)],
        compiler_params=params,
        cost_estimate=pl.CostEstimate(flops=8 * 10**9, bytes_accessed=10**7, transcendentals=0),
        name="local",
    )(norms, low, qs, own)
    late, acc = lax.optimization_barrier((own, acc))
    three = lax.ppermute(late, "cp", [(i, i + 3) for i in range(1, cp - 3, 2)])
    two, acc = lax.optimization_barrier((two, acc))
    two_flip = lax.ppermute(two, "cp", flip_route)
    whole = pl.BlockSpec(size, lambda i: (0, 0, 0))
    return pl.pallas_call(
        functools.partial(far_kernel, group),
        grid=(steps,),
        in_specs=[
            smem,
            vmem,
            pl.BlockSpec((kv_heads, lanes, width), lambda i: (0, i, 0)),
            pl.BlockSpec((kv_heads, sums + 8, lanes), lambda i: (0, 0, i)),
        ]
        + [whole] * 4,
        out_specs=pl.BlockSpec((TILE, q_heads, width), lambda i: (i, 0, 0)),
        out_shape=jax.ShapeDtypeStruct(queries.shape, jnp.bfloat16),
        scratch_shapes=[
            pltpu.VMEM((kv_heads, (WIN - 1) * rows, width), jnp.bfloat16),
            pltpu.VMEM((kv_heads, WIN - 1, sums, rows), jnp.bfloat16),
            pltpu.VMEM((kv_heads, sums + 8, lanes), jnp.float32),
            pltpu.SMEM((WIN,), jnp.int32),
            pltpu.SMEM((1,), jnp.float32),
        ],
        compiler_params=params,
        cost_estimate=pl.CostEstimate(flops=2 * 10**10, bytes_accessed=10**7, transcendentals=0),
        name="far",
    )(norms, tag, qs, acc, flip, two, two_flip, three)


def solution(mesh):
    in_specs = (
        P("cp", "tp", None),
        P(("cp", "tp"), None, None),
        P(("cp", "tp"), None, None),
        P("cp"),
    )
    out_specs = P("cp", "tp", None)
    return jax.shard_map(shards, mesh=mesh, in_specs=in_specs, out_specs=out_specs, check_vma=False)
```

```python
import functools
import math

import jax
import jax.numpy as jnp
from jax import lax
from jax.experimental import pallas as pl
from jax.experimental.pallas import tpu as pltpu
from jax.sharding import PartitionSpec as P

WIN = 4
NT = (((1,), (1,)), ((), ()))
LOG2E = 1.4426950408889634
SAFE = 100.0
NEG = -1e30
TILE = 256
SMALL = 256
PAD = 16
VMEM_LIMIT = 48 * 2**20


def top_norm(x):
    xf = x.astype(jnp.float32)
    return jnp.max(jnp.sum(xf * xf, axis=-1, keepdims=True))


def pack_kernel(tp, kv_heads, k_ref, v_ref, *refs):
    out_refs, buf = refs[:-1], refs[-1]
    part, width = buf.shape[1], k_ref.shape[1]
    heads = k_ref.shape[0] // part
    n = 16 * heads
    row = lax.broadcasted_iota(jnp.int32, (n, n), 0)
    col = lax.broadcasted_iota(jnp.int32, (n, n), 1)
    swap = (col == (row % 16) * heads + row // 16).astype(jnp.bfloat16)
    for which, ref in enumerate((k_ref, v_ref)):
        for c in range(part // 16):
            y = jnp.dot(swap, ref[c * n : (c + 1) * n], preferred_element_type=jnp.float32)
            y = y.astype(jnp.bfloat16)
            for h in range(heads):
                at = (2 * (h % kv_heads) + which) * width
                buf[h // kv_heads, c * 16 : c * 16 + 16, at : at + width] = y[16 * h : 16 * h + 16]
    me = lax.axis_index("tp")
    for d in range(tp):
        out_refs[d][...] = buf[lax.rem(me + d, tp)]


def scale_kernel(group, low_ref, q_ref, qs_ref, norm_ref):
    step = pl.program_id(0)
    tokens, heads, width = q_ref.shape
    qf = q_ref[...].astype(jnp.float32) * (LOG2E / math.sqrt(width))
    top = jnp.float32(0.0)
    for g in range(heads // group):
        x = qf[:, group * g : group * (g + 1)].reshape(tokens * group, width)
        qs_ref[g] = x.astype(jnp.bfloat16)
        top = jnp.maximum(top, top_norm(x))
    norm_ref[step] = top * 1.02


def assemble_kernel(tp, kv_heads, norm_ref, tag_ref, *refs):
    parts, o_ref, v_ref = refs[:tp], refs[tp], refs[tp + 1]
    part, width = parts[0].shape[0], v_ref.shape[1]
    rows = part * tp
    me = lax.axis_index("tp")
    for g in range(kv_heads):
        for d in range(tp):
            at = pl.multiple_of(lax.rem(me + tp - d, tp) * part, 16)
            o_ref[g, pl.ds(at, part)] = parts[d][:, 2 * width * g : 2 * width * g + width]
            v_ref[pl.ds(at, part)] = parts[d][:, 2 * width * g + width : 2 * width * (g + 1)].astype(jnp.float32)
        for j in range(rows // width):
            block = v_ref[j * width : (j + 1) * width].T
            o_ref[g, rows + j * width : rows + (j + 1) * width] = block.astype(jnp.bfloat16)
        o_ref[g, 2 * rows : 2 * rows + PAD] = tag_ref[...]
        top = top_norm(o_ref[g, :rows]) * 1.02
        o_ref[g, 2 * rows + PAD :] = jnp.full((PAD, width), top, jnp.float32).astype(jnp.bfloat16)


def fill_values(vt_ref, at, kv_ref, g, rows, count):
    width = kv_ref.shape[-1]
    more = vt_ref.shape[-2] - width
    for j in range(rows // width):
        cols = slice(j * width, (j + 1) * width)
        valid = j * width + lax.broadcasted_iota(jnp.int32, (1, width), 1) >= rows - count
        vt = kv_ref[g, rows + j * width : rows + (j + 1) * width].astype(jnp.float32)
        vt_ref[(*at, slice(0, width), cols)] = jnp.where(valid, vt, 0.0).astype(jnp.bfloat16)
        ones = jnp.ones((more, width), jnp.float32)
        vt_ref[(*at, slice(width, width + more), cols)] = jnp.where(valid, ones, 0.0).astype(jnp.bfloat16)


def general_tile(acc_ref, g, s, ok, vt):
    sums = vt.shape[0]
    old = acc_ref[g, sums : sums + 1]
    m = jnp.maximum(old, jnp.max(jnp.where(ok, s, NEG), axis=0, keepdims=True))
    p = jnp.where(ok, jnp.exp2(s - m), 0.0).astype(jnp.bfloat16)
    o = jnp.dot(vt, p, preferred_element_type=jnp.float32)
    acc_ref[g, :sums] = acc_ref[g, :sums] * jnp.exp2(old - m) + o
    acc_ref[g, sums:] = jnp.broadcast_to(m, (8, s.shape[1]))


def local_kernel(group, norm_ref, low_ref, qs_ref, own_ref, acc_ref, vt_ref):
    step = pl.program_id(1)
    width = own_ref.shape[2]
    rows = vt_ref.shape[1]
    sums = vt_ref.shape[0]
    lanes = TILE * group

    @pl.when(step == 0)
    def _():
        fill_values(vt_ref, (), own_ref, 0, rows, rows)

    kn = jnp.max(own_ref[0, 2 * rows + PAD :].astype(jnp.float32))
    fast = norm_ref[step] * kn <= SAFE * abs(SAFE)
    token = step * TILE + lax.broadcasted_iota(jnp.int32, (1, lanes), 1) // group
    low = low_ref[0:1]

    for i in range(rows // TILE):

        @pl.when(fast & (step == i))
        def _():
            keys = (i + 1) * TILE
            s = lax.dot_general(own_ref[0, :keys], qs_ref[0], NT, preferred_element_type=jnp.float32)
            at = lax.broadcasted_iota(jnp.int32, (keys, lanes), 0)
            p = jnp.where((at >= low) & (at <= token), jnp.exp2(s), 0.0).astype(jnp.bfloat16)
            acc_ref[0, :sums] = jnp.dot(vt_ref[:, :keys], p, preferred_element_type=jnp.float32)
            acc_ref[0, sums:] = jnp.zeros((8, lanes), jnp.float32)

    @pl.when(jnp.logical_not(fast))
    def _():
        acc_ref[0, :sums] = jnp.zeros((sums, lanes), jnp.float32)
        acc_ref[0, sums:] = jnp.full((8, lanes), NEG, jnp.float32)

        def tile(j, carry):
            at = pl.multiple_of(j * SMALL, SMALL)
            s = lax.dot_general(own_ref[0, pl.ds(at, SMALL)], qs_ref[0], NT, preferred_element_type=jnp.float32)
            pos = at + lax.broadcasted_iota(jnp.int32, (SMALL, lanes), 0)
            general_tile(acc_ref, 0, s, (pos >= low) & (pos <= token), vt_ref[:, pl.ds(at, SMALL)])
            return carry

        lax.fori_loop(0, ((step + 1) * TILE + SMALL - 1) // SMALL, tile, 0)


def far_kernel(group, last, norm_ref, tag_ref, qs_ref, acc_in_ref, *refs):
    if last:
        near_ref, other_ref, o_ref, k_ref, vt_ref, acc_ref, n_ref, kn_ref = refs
    else:
        near_ref, other_ref, acc_ref, k_ref, vt_ref, n_ref, kn_ref = refs
    step = pl.program_id(0)
    kv_heads, lanes, width = qs_ref.shape
    rows = vt_ref.shape[-1]
    sums = vt_ref.shape[-2]

    @pl.when(step == 0)
    def _():
        odd = lax.rem(lax.axis_index("cp"), 2) == 1
        own = tag_ref[...].astype(jnp.float32)
        at = lax.broadcasted_iota(jnp.int32, own.shape, 0) * width
        at = at + lax.broadcasted_iota(jnp.int32, own.shape, 1)
        first = jnp.max(jnp.where(at == 0, own, 0.0))
        count = lambda x: jnp.sum((x.astype(jnp.float32) == first).astype(jnp.float32)).astype(jnp.int32)
        same = lambda ref: count(ref[0, 2 * rows : 2 * rows + PAD])
        n_ref[0] = same(other_ref)
        n_ref[1] = jnp.where(odd != last, same(near_ref), 0)
        n_ref[2] = count(own)
        kn_ref[0] = 0.0
        for slot, ref in ((0, other_ref), (1, near_ref)):

            @pl.when(n_ref[slot] > 0)
            def _():
                for g in range(kv_heads):
                    k_ref[g, slot * rows : (slot + 1) * rows] = ref[g, :rows]
                    fill_values(vt_ref, (g, slot), ref, g, rows, n_ref[slot])
                    kn_ref[0] = jnp.maximum(kn_ref[0], jnp.max(ref[g, 2 * rows + PAD :].astype(jnp.float32)))

    acc_ref[...] = acc_in_ref[...]
    reach = n_ref[2]
    fast = norm_ref[step] * kn_ref[0] <= SAFE * abs(SAFE)
    for g in range(kv_heads):
        fast = fast & (jnp.max(jnp.abs(acc_in_ref[g, sums:])) == 0.0)
    token = step * TILE + lax.broadcasted_iota(jnp.int32, (1, lanes), 1) // group
    mine = token < reach
    some = step * TILE < reach

    def scores(g, at, keys):
        return lax.dot_general(k_ref[g, pl.ds(at, keys)], qs_ref[g], NT, preferred_element_type=jnp.float32)

    def block(j, carry):
        g = lax.rem(j, kv_heads)
        slot = j // kv_heads
        p = jnp.exp2(scores(g, pl.multiple_of(slot * rows, rows), rows)).astype(jnp.bfloat16)
        o = jnp.dot(vt_ref[g, slot], p, preferred_element_type=jnp.float32)
        acc_ref[g, :sums] += jnp.where(mine, o, 0.0)
        return carry

    def tile(j, carry):
        g = lax.rem(j, kv_heads)
        at = pl.multiple_of(j // kv_heads * SMALL, SMALL)
        p = jnp.exp2(scores(g, at, SMALL)).astype(jnp.bfloat16)
        o = jnp.dot(vt_ref[g, 0, :, pl.ds(at, SMALL)], p, preferred_element_type=jnp.float32)
        acc_ref[g, :sums] += jnp.where(mine, o, 0.0)
        return carry

    @pl.when(fast & some)
    def _():
        whole = 1 if last else jnp.where(n_ref[0] > 0, 0, 1)
        lax.fori_loop(whole * kv_heads, jnp.where(n_ref[1] > 0, 2, 1) * kv_heads, block, 0)
        if last:
            lax.fori_loop((rows - n_ref[0]) // SMALL * kv_heads, rows // SMALL * kv_heads, tile, 0)

    @pl.when(jnp.logical_not(fast) & some)
    def _():
        def general(j, carry):
            g = lax.rem(j, kv_heads)
            at = pl.multiple_of(j // kv_heads * SMALL, SMALL)
            slot = at // rows
            s = scores(g, at, SMALL)
            pos = at + lax.broadcasted_iota(jnp.int32, (SMALL, lanes), 0)
            ok = (pos >= (slot + 1) * rows - n_ref[slot]) & mine
            vt = vt_ref[g, slot, :, pl.ds(pl.multiple_of(at - slot * rows, SMALL), SMALL)]
            general_tile(acc_ref, g, s, ok, vt)
            return carry

        for slot in range(2):
            end = (slot + 1) * rows
            lax.fori_loop((end - n_ref[slot]) // SMALL * kv_heads, end // SMALL * kv_heads, general, 0)

    if last:
        outs = []
        for g in range(kv_heads):
            o = acc_ref[g, :width] * (1.0 / acc_ref[g, width : width + 1])
            outs.append(o.T.reshape(TILE, group, width))
        o_ref[...] = jnp.concatenate(outs, axis=1).astype(jnp.bfloat16)


def shards(queries, key_states, value_states, doc_ids):
    rows, q_heads, width = queries.shape
    tp = lax.axis_size("tp")
    cp = lax.axis_size("cp")
    part, heads = key_states.shape[:2]
    kv_heads = heads // tp
    group = q_heads // kv_heads
    lanes = TILE * group
    steps = rows // TILE
    params = pltpu.CompilerParams(vmem_limit_bytes=VMEM_LIMIT)
    vmem = pl.BlockSpec(memory_space=pltpu.VMEM)
    smem = pl.BlockSpec(memory_space=pltpu.SMEM)

    tag = (doc_ids + 1).astype(jnp.bfloat16).reshape(rows // width, width)
    tag = jnp.pad(tag, ((0, PAD - tag.shape[0]), (0, 0)))
    low = jnp.sum((doc_ids[None, :] < doc_ids[:, None]).astype(jnp.int32), axis=1)
    low = jnp.broadcast_to(jnp.repeat(low, group)[None], (8, rows * group))

    pieces = pl.pallas_call(
        functools.partial(pack_kernel, tp, kv_heads),
        in_specs=[vmem, vmem],
        out_specs=[vmem] * tp,
        out_shape=[jax.ShapeDtypeStruct((part, 2 * kv_heads * width), jnp.bfloat16)] * tp,
        scratch_shapes=[pltpu.VMEM((tp, part, 2 * kv_heads * width), jnp.bfloat16)],
        compiler_params=params,
        name="pack",
    )(key_states.reshape(part * heads, width), value_states.reshape(part * heads, width))
    mine = [pieces[0]]
    for d in range(1, tp):
        mine.append(lax.ppermute(pieces[d], "tp", [(i, (i + d) % tp) for i in range(tp)]))

    qs, norms = pl.pallas_call(
        functools.partial(scale_kernel, group),
        grid=(steps,),
        in_specs=[pl.BlockSpec(memory_space=pl.ANY), pl.BlockSpec((TILE, q_heads, width), lambda i: (i, 0, 0))],
        out_specs=[pl.BlockSpec((kv_heads, lanes, width), lambda i: (0, i, 0)), smem],
        out_shape=[
            jax.ShapeDtypeStruct((kv_heads, rows * group, width), jnp.bfloat16),
            jax.ShapeDtypeStruct((steps,), jnp.float32),
        ],
        compiler_params=params,
        name="scale",
    )(low, queries)
    size = (kv_heads, 2 * rows + 2 * PAD, width)
    own = pl.pallas_call(
        functools.partial(assemble_kernel, tp, kv_heads),
        in_specs=[smem] + [vmem] * (tp + 1),
        out_specs=vmem,
        out_shape=jax.ShapeDtypeStruct(size, jnp.bfloat16),
        scratch_shapes=[pltpu.VMEM((rows, width), jnp.float32)],
        compiler_params=params,
        name="assemble",
    )(norms, tag, *mine)

    flip_route = [(i, i ^ 1) for i in range(cp)]
    two = lax.ppermute(own, "cp", [(i, i + 2) for i in range(cp - 2)])
    flip = lax.ppermute(own, "cp", flip_route)

    sums = width + 16
    acc = pl.pallas_call(
        functools.partial(local_kernel, group),
        grid=(kv_heads, steps),
        in_specs=[
            smem,
            pl.BlockSpec((8, lanes), lambda g, i: (0, i)),
            pl.BlockSpec((1, lanes, width), lambda g, i: (g, i, 0)),
            pl.BlockSpec((1, *size[1:]), lambda g, i: (g, 0, 0)),
        ],
        out_specs=pl.BlockSpec((1, sums + 8, lanes), lambda g, i: (g, 0, i)),
        out_shape=jax.ShapeDtypeStruct((kv_heads, sums + 8, rows * group), jnp.float32),
        scratch_shapes=[pltpu.VMEM((sums, rows), jnp.bfloat16)],
        compiler_params=params,
        cost_estimate=pl.CostEstimate(flops=8 * 10**9, bytes_accessed=10**7, transcendentals=0),
        name="local",
    )(norms, low, qs, own)
    two, acc = lax.optimization_barrier((two, acc))
    near = lax.ppermute(two, "cp", [(i, i - 1) for i in range(1, cp, 2)])
    three = lax.ppermute(two, "cp", [(i, i + 1) for i in range(cp - 1)])
    whole = pl.BlockSpec(size, lambda i: (0, 0, 0))
    acc_spec = pl.BlockSpec((kv_heads, sums + 8, lanes), lambda i: (0, 0, i))
    in_specs = [smem, vmem, pl.BlockSpec((kv_heads, lanes, width), lambda i: (0, i, 0)), acc_spec]
    slots = lambda blocks: [
        pltpu.VMEM((kv_heads, blocks * rows, width), jnp.bfloat16),
        pltpu.VMEM((kv_heads, blocks, sums, rows), jnp.bfloat16),
    ]
    scalars = [pltpu.SMEM((WIN,), jnp.int32), pltpu.SMEM((1,), jnp.float32)]
    acc = pl.pallas_call(
        functools.partial(far_kernel, group, False),
        grid=(steps,),
        in_specs=in_specs + [whole] * 2,
        out_specs=acc_spec,
        out_shape=jax.ShapeDtypeStruct(acc.shape, jnp.float32),
        scratch_shapes=[*slots(2), *scalars],
        compiler_params=params,
        cost_estimate=pl.CostEstimate(flops=2 * 10**10, bytes_accessed=10**7, transcendentals=0),
        name="near",
    )(norms, tag, qs, acc, flip, two)
    return pl.pallas_call(
        functools.partial(far_kernel, group, True),
        grid=(steps,),
        in_specs=in_specs + [whole] * 2,
        out_specs=pl.BlockSpec((TILE, q_heads, width), lambda i: (i, 0, 0)),
        out_shape=jax.ShapeDtypeStruct(queries.shape, jnp.bfloat16),
        scratch_shapes=[*slots(2), pltpu.VMEM((kv_heads, sums + 8, lanes), jnp.float32), *scalars],
        compiler_params=params,
        name="last",
    )(norms, tag, qs, acc, near, three)


def solution(mesh):
    in_specs = (
        P("cp", "tp", None),
        P(("cp", "tp"), None, None),
        P(("cp", "tp"), None, None),
        P("cp"),
    )
    out_specs = P("cp", "tp", None)
    return jax.shard_map(shards, mesh=mesh, in_specs=in_specs, out_specs=out_specs, check_vma=False)
```

```python
import functools
import math

import jax
import jax.numpy as jnp
from jax import lax
from jax.experimental import pallas as pl
from jax.experimental.pallas import tpu as pltpu
from jax.sharding import PartitionSpec as P

WIN = 4
NT = (((1,), (1,)), ((), ()))
LOG2E = 1.4426950408889634
SAFE = 100.0
NEG = -1e30
TILE = 256
SMALL = 256
PAD = 16
VMEM_LIMIT = 34 * 2**20


def top_norm(x):
    xf = x.astype(jnp.float32)
    return jnp.max(jnp.sum(xf * xf, axis=-1, keepdims=True))


def pack_kernel(tp, kv_heads, k_ref, v_ref, *refs):
    out_refs, buf = refs[:-1], refs[-1]
    part, width = buf.shape[1], k_ref.shape[1]
    heads = k_ref.shape[0] // part
    n = 16 * heads
    row = lax.broadcasted_iota(jnp.int32, (n, n), 0)
    col = lax.broadcasted_iota(jnp.int32, (n, n), 1)
    swap = (col == (row % 16) * heads + row // 16).astype(jnp.bfloat16)
    for which, ref in enumerate((k_ref, v_ref)):
        for c in range(part // 16):
            y = jnp.dot(swap, ref[c * n : (c + 1) * n], preferred_element_type=jnp.float32)
            y = y.astype(jnp.bfloat16)
            for h in range(heads):
                at = (2 * (h % kv_heads) + which) * width
                buf[h // kv_heads, c * 16 : c * 16 + 16, at : at + width] = y[16 * h : 16 * h + 16]
    me = lax.axis_index("tp")
    for d in range(tp):
        out_refs[d][...] = buf[lax.rem(me + d, tp)]


def scale_kernel(group, low_ref, q_ref, qs_ref, norm_ref):
    step = pl.program_id(0)
    tokens, heads, width = q_ref.shape
    qf = q_ref[...].astype(jnp.float32) * (LOG2E / math.sqrt(width))
    top = jnp.float32(0.0)
    for g in range(heads // group):
        x = qf[:, group * g : group * (g + 1)].reshape(tokens * group, width)
        qs_ref[g] = x.astype(jnp.bfloat16)
        top = jnp.maximum(top, top_norm(x))
    norm_ref[step] = top * 1.02


def assemble_kernel(tp, kv_heads, norm_ref, tag_ref, *refs):
    parts, o_ref, v_ref = refs[:tp], refs[tp], refs[tp + 1]
    part, width = parts[0].shape[0], v_ref.shape[1]
    rows = part * tp
    me = lax.axis_index("tp")
    for g in range(kv_heads):
        for d in range(tp):
            at = pl.multiple_of(lax.rem(me + tp - d, tp) * part, 16)
            o_ref[g, pl.ds(at, part)] = parts[d][:, 2 * width * g : 2 * width * g + width]
            v_ref[pl.ds(at, part)] = parts[d][:, 2 * width * g + width : 2 * width * (g + 1)].astype(jnp.float32)
        for j in range(rows // width):
            block = v_ref[j * width : (j + 1) * width].T
            o_ref[g, rows + j * width : rows + (j + 1) * width] = block.astype(jnp.bfloat16)
        o_ref[g, 2 * rows : 2 * rows + PAD] = tag_ref[...]
        top = top_norm(o_ref[g, :rows]) * 1.02
        o_ref[g, 2 * rows + PAD :] = jnp.full((PAD, width), top, jnp.float32).astype(jnp.bfloat16)


def fill_values(vt_ref, at, kv_ref, g, rows, count):
    width = kv_ref.shape[-1]
    more = vt_ref.shape[-2] - width
    for j in range(rows // width):
        cols = slice(j * width, (j + 1) * width)
        valid = j * width + lax.broadcasted_iota(jnp.int32, (1, width), 1) >= rows - count
        vt = kv_ref[g, rows + j * width : rows + (j + 1) * width].astype(jnp.float32)
        vt_ref[(*at, slice(0, width), cols)] = jnp.where(valid, vt, 0.0).astype(jnp.bfloat16)
        ones = jnp.ones((more, width), jnp.float32)
        vt_ref[(*at, slice(width, width + more), cols)] = jnp.where(valid, ones, 0.0).astype(jnp.bfloat16)


def general_tile(acc_ref, g, s, ok, vt):
    sums = vt.shape[0]
    old = acc_ref[g, sums : sums + 1]
    m = jnp.maximum(old, jnp.max(jnp.where(ok, s, NEG), axis=0, keepdims=True))
    p = jnp.where(ok, jnp.exp2(s - m), 0.0).astype(jnp.bfloat16)
    o = jnp.dot(vt, p, preferred_element_type=jnp.float32)
    acc_ref[g, :sums] = acc_ref[g, :sums] * jnp.exp2(old - m) + o
    acc_ref[g, sums:] = jnp.broadcast_to(m, (8, s.shape[1]))


def local_kernel(group, norm_ref, low_ref, qs_ref, own_ref, acc_ref, vt_ref):
    step = pl.program_id(1)
    width = own_ref.shape[2]
    rows = vt_ref.shape[1]
    sums = vt_ref.shape[0]
    lanes = TILE * group

    @pl.when(step == 0)
    def _():
        fill_values(vt_ref, (), own_ref, 0, rows, rows)

    kn = jnp.max(own_ref[0, 2 * rows + PAD :].astype(jnp.float32))
    fast = norm_ref[step] * kn <= SAFE * abs(SAFE)
    token = step * TILE + lax.broadcasted_iota(jnp.int32, (1, lanes), 1) // group
    low = low_ref[0:1]

    for i in range(rows // TILE):

        @pl.when(fast & (step == i))
        def _():
            keys = (i + 1) * TILE
            s = lax.dot_general(own_ref[0, :keys], qs_ref[0], NT, preferred_element_type=jnp.float32)
            at = lax.broadcasted_iota(jnp.int32, (keys, lanes), 0)
            p = jnp.where((at >= low) & (at <= token), jnp.exp2(s), 0.0).astype(jnp.bfloat16)
            acc_ref[0, :sums] = jnp.dot(vt_ref[:, :keys], p, preferred_element_type=jnp.float32)
            acc_ref[0, sums:] = jnp.zeros((8, lanes), jnp.float32)

    @pl.when(jnp.logical_not(fast))
    def _():
        acc_ref[0, :sums] = jnp.zeros((sums, lanes), jnp.float32)
        acc_ref[0, sums:] = jnp.full((8, lanes), NEG, jnp.float32)

        def tile(j, carry):
            at = pl.multiple_of(j * SMALL, SMALL)
            s = lax.dot_general(own_ref[0, pl.ds(at, SMALL)], qs_ref[0], NT, preferred_element_type=jnp.float32)
            pos = at + lax.broadcasted_iota(jnp.int32, (SMALL, lanes), 0)
            general_tile(acc_ref, 0, s, (pos >= low) & (pos <= token), vt_ref[:, pl.ds(at, SMALL)])
            return carry

        lax.fori_loop(0, ((step + 1) * TILE + SMALL - 1) // SMALL, tile, 0)


def far_kernel(group, last, norm_ref, tag_ref, qs_ref, acc_in_ref, *refs):
    if last:
        near_ref, other_ref, o_ref, k_ref, vt_ref, acc_ref, n_ref, kn_ref = refs
    else:
        near_ref, other_ref, acc_ref, k_ref, vt_ref, n_ref, kn_ref = refs
    step = pl.program_id(0)
    kv_heads, lanes, width = qs_ref.shape
    rows = vt_ref.shape[-1]
    sums = vt_ref.shape[-2]

    @pl.when(step == 0)
    def _():
        odd = lax.rem(lax.axis_index("cp"), 2) == 1
        own = tag_ref[...].astype(jnp.float32)
        at = lax.broadcasted_iota(jnp.int32, own.shape, 0) * width
        at = at + lax.broadcasted_iota(jnp.int32, own.shape, 1)
        first = jnp.max(jnp.where(at == 0, own, 0.0))
        count = lambda x: jnp.sum((x.astype(jnp.float32) == first).astype(jnp.float32)).astype(jnp.int32)
        same = lambda ref: count(ref[0, 2 * rows : 2 * rows + PAD])
        n_ref[0] = same(other_ref)
        n_ref[1] = jnp.where(odd != last, same(near_ref), 0)
        n_ref[2] = count(own)
        kn_ref[0] = 0.0
        for slot, ref in ((0, other_ref), (1, near_ref)):

            @pl.when(n_ref[slot] > 0)
            def _():
                for g in range(kv_heads):
                    k_ref[g, slot * rows : (slot + 1) * rows] = ref[g, :rows]
                    fill_values(vt_ref, (g, slot), ref, g, rows, n_ref[slot])
                    kn_ref[0] = jnp.maximum(kn_ref[0], jnp.max(ref[g, 2 * rows + PAD :].astype(jnp.float32)))

    acc_ref[...] = acc_in_ref[...]
    reach = n_ref[2]
    fast = norm_ref[step] * kn_ref[0] <= SAFE * abs(SAFE)
    for g in range(kv_heads):
        fast = fast & (jnp.max(jnp.abs(acc_in_ref[g, sums:])) == 0.0)
    token = step * TILE + lax.broadcasted_iota(jnp.int32, (1, lanes), 1) // group
    mine = token < reach
    some = step * TILE < reach

    def scores(g, at, keys):
        return lax.dot_general(k_ref[g, pl.ds(at, keys)], qs_ref[g], NT, preferred_element_type=jnp.float32)

    def block(j, carry):
        g = lax.rem(j, kv_heads)
        slot = j // kv_heads
        p = jnp.exp2(scores(g, pl.multiple_of(slot * rows, rows), rows)).astype(jnp.bfloat16)
        o = jnp.dot(vt_ref[g, slot], p, preferred_element_type=jnp.float32)
        acc_ref[g, :sums] += jnp.where(mine, o, 0.0)
        return carry

    def tile(j, carry):
        g = lax.rem(j, kv_heads)
        at = pl.multiple_of(j // kv_heads * SMALL, SMALL)
        p = jnp.exp2(scores(g, at, SMALL)).astype(jnp.bfloat16)
        o = jnp.dot(vt_ref[g, 0, :, pl.ds(at, SMALL)], p, preferred_element_type=jnp.float32)
        acc_ref[g, :sums] += jnp.where(mine, o, 0.0)
        return carry

    @pl.when(fast & some)
    def _():
        whole = 1 if last else jnp.where(n_ref[0] > 0, 0, 1)
        lax.fori_loop(whole * kv_heads, jnp.where(n_ref[1] > 0, 2, 1) * kv_heads, block, 0)
        if last:
            lax.fori_loop((rows - n_ref[0]) // SMALL * kv_heads, rows // SMALL * kv_heads, tile, 0)

    @pl.when(jnp.logical_not(fast) & some)
    def _():
        def general(j, carry):
            g = lax.rem(j, kv_heads)
            at = pl.multiple_of(j // kv_heads * SMALL, SMALL)
            slot = at // rows
            s = scores(g, at, SMALL)
            pos = at + lax.broadcasted_iota(jnp.int32, (SMALL, lanes), 0)
            ok = (pos >= (slot + 1) * rows - n_ref[slot]) & mine
            vt = vt_ref[g, slot, :, pl.ds(pl.multiple_of(at - slot * rows, SMALL), SMALL)]
            general_tile(acc_ref, g, s, ok, vt)
            return carry

        for slot in range(2):
            end = (slot + 1) * rows
            lax.fori_loop((end - n_ref[slot]) // SMALL * kv_heads, end // SMALL * kv_heads, general, 0)

    if last:
        outs = []
        for g in range(kv_heads):
            o = acc_ref[g, :width] * (1.0 / acc_ref[g, width : width + 1])
            outs.append(o.T.reshape(TILE, group, width))
        o_ref[...] = jnp.concatenate(outs, axis=1).astype(jnp.bfloat16)


def shards(queries, key_states, value_states, doc_ids):
    rows, q_heads, width = queries.shape
    tp = lax.axis_size("tp")
    cp = lax.axis_size("cp")
    part, heads = key_states.shape[:2]
    kv_heads = heads // tp
    group = q_heads // kv_heads
    lanes = TILE * group
    steps = rows // TILE
    params = pltpu.CompilerParams(vmem_limit_bytes=VMEM_LIMIT)
    vmem = pl.BlockSpec(memory_space=pltpu.VMEM)
    smem = pl.BlockSpec(memory_space=pltpu.SMEM)

    tag = (doc_ids + 1).astype(jnp.bfloat16).reshape(rows // width, width)
    tag = jnp.pad(tag, ((0, PAD - tag.shape[0]), (0, 0)))
    low = jnp.sum((doc_ids[None, :] < doc_ids[:, None]).astype(jnp.int32), axis=1)
    low = jnp.broadcast_to(jnp.repeat(low, group)[None], (8, rows * group))

    pieces = pl.pallas_call(
        functools.partial(pack_kernel, tp, kv_heads),
        in_specs=[vmem, vmem],
        out_specs=[vmem] * tp,
        out_shape=[jax.ShapeDtypeStruct((part, 2 * kv_heads * width), jnp.bfloat16)] * tp,
        scratch_shapes=[pltpu.VMEM((tp, part, 2 * kv_heads * width), jnp.bfloat16)],
        compiler_params=params,
        name="pack",
    )(key_states.reshape(part * heads, width), value_states.reshape(part * heads, width))
    mine = [pieces[0]]
    for d in range(1, tp):
        mine.append(lax.ppermute(pieces[d], "tp", [(i, (i + d) % tp) for i in range(tp)]))

    qs, norms = pl.pallas_call(
        functools.partial(scale_kernel, group),
        grid=(steps,),
        in_specs=[pl.BlockSpec(memory_space=pl.ANY), pl.BlockSpec((TILE, q_heads, width), lambda i: (i, 0, 0))],
        out_specs=[pl.BlockSpec((kv_heads, lanes, width), lambda i: (0, i, 0)), smem],
        out_shape=[
            jax.ShapeDtypeStruct((kv_heads, rows * group, width), jnp.bfloat16),
            jax.ShapeDtypeStruct((steps,), jnp.float32),
        ],
        compiler_params=params,
        name="scale",
    )(low, queries)
    size = (kv_heads, 2 * rows + 2 * PAD, width)
    own = pl.pallas_call(
        functools.partial(assemble_kernel, tp, kv_heads),
        in_specs=[smem] + [vmem] * (tp + 1),
        out_specs=vmem,
        out_shape=jax.ShapeDtypeStruct(size, jnp.bfloat16),
        scratch_shapes=[pltpu.VMEM((rows, width), jnp.float32)],
        compiler_params=params,
        name="assemble",
    )(norms, tag, *mine)

    flip_route = [(i, i ^ 1) for i in range(cp)]
    two = lax.ppermute(own, "cp", [(i, i + 2) for i in range(cp - 2)])
    flip = lax.ppermute(own, "cp", flip_route)

    sums = width + 16
    acc = pl.pallas_call(
        functools.partial(local_kernel, group),
        grid=(kv_heads, steps),
        in_specs=[
            smem,
            pl.BlockSpec((8, lanes), lambda g, i: (0, i)),
            pl.BlockSpec((1, lanes, width), lambda g, i: (g, i, 0)),
            pl.BlockSpec((1, *size[1:]), lambda g, i: (g, 0, 0)),
        ],
        out_specs=pl.BlockSpec((1, sums + 8, lanes), lambda g, i: (g, 0, i)),
        out_shape=jax.ShapeDtypeStruct((kv_heads, sums + 8, rows * group), jnp.float32),
        scratch_shapes=[pltpu.VMEM((sums, rows), jnp.bfloat16)],
        compiler_params=params,
        cost_estimate=pl.CostEstimate(flops=8 * 10**9, bytes_accessed=10**7, transcendentals=0),
        name="local",
    )(norms, low, qs, own)
    two, acc = lax.optimization_barrier((two, acc))
    near = lax.ppermute(two, "cp", [(i, i - 1) for i in range(1, cp, 2)])
    three = lax.ppermute(two, "cp", [(i, i + 1) for i in range(cp - 1)])
    whole = pl.BlockSpec(size, lambda i: (0, 0, 0))
    acc_spec = pl.BlockSpec((kv_heads, sums + 8, lanes), lambda i: (0, 0, i))
    in_specs = [smem, vmem, pl.BlockSpec((kv_heads, lanes, width), lambda i: (0, i, 0)), acc_spec]
    slots = lambda blocks: [
        pltpu.VMEM((kv_heads, blocks * rows, width), jnp.bfloat16),
        pltpu.VMEM((kv_heads, blocks, sums, rows), jnp.bfloat16),
    ]
    scalars = [pltpu.SMEM((WIN,), jnp.int32), pltpu.SMEM((1,), jnp.float32)]
    acc = pl.pallas_call(
        functools.partial(far_kernel, group, False),
        grid=(steps,),
        in_specs=in_specs + [whole] * 2,
        out_specs=acc_spec,
        out_shape=jax.ShapeDtypeStruct(acc.shape, jnp.float32),
        scratch_shapes=[*slots(2), *scalars],
        compiler_params=params,
        cost_estimate=pl.CostEstimate(flops=2 * 10**10, bytes_accessed=10**7, transcendentals=0),
        name="near",
    )(norms, tag, qs, acc, flip, two)
    return pl.pallas_call(
        functools.partial(far_kernel, group, True),
        grid=(steps,),
        in_specs=in_specs + [whole] * 2,
        out_specs=pl.BlockSpec((TILE, q_heads, width), lambda i: (i, 0, 0)),
        out_shape=jax.ShapeDtypeStruct(queries.shape, jnp.bfloat16),
        scratch_shapes=[*slots(2), pltpu.VMEM((kv_heads, sums + 8, lanes), jnp.float32), *scalars],
        compiler_params=params,
        name="last",
    )(norms, tag, qs, acc, near, three)


def solution(mesh):
    in_specs = (
        P("cp", "tp", None),
        P(("cp", "tp"), None, None),
        P(("cp", "tp"), None, None),
        P("cp"),
    )
    out_specs = P("cp", "tp", None)
    return jax.shard_map(shards, mesh=mesh, in_specs=in_specs, out_specs=out_specs, check_vma=False)
```

```python
import functools
import math

import jax
import jax.numpy as jnp
from jax import lax
from jax.experimental import pallas as pl
from jax.experimental.pallas import tpu as pltpu
from jax.sharding import PartitionSpec as P

WIN = 4
NT = (((1,), (1,)), ((), ()))
LOG2E = 1.4426950408889634
SAFE = 100.0
NEG = -1e30
TILE = 256
SMALL = 256
PAD = 16
VMEM_LIMIT = 34 * 2**20


def top_norm(x):
    xf = x.astype(jnp.float32)
    return jnp.max(jnp.sum(xf * xf, axis=-1, keepdims=True))


def pack_kernel(tp, kv_heads, k_ref, v_ref, *refs):
    out_refs, buf = refs[:-1], refs[-1]
    part, width = buf.shape[1], k_ref.shape[1]
    heads = k_ref.shape[0] // part
    n = 16 * heads
    row = lax.broadcasted_iota(jnp.int32, (n, n), 0)
    col = lax.broadcasted_iota(jnp.int32, (n, n), 1)
    swap = (col == (row % 16) * heads + row // 16).astype(jnp.bfloat16)
    for which, ref in enumerate((k_ref, v_ref)):
        for c in range(part // 16):
            y = jnp.dot(swap, ref[c * n : (c + 1) * n], preferred_element_type=jnp.float32)
            y = y.astype(jnp.bfloat16)
            for h in range(heads):
                at = (2 * (h % kv_heads) + which) * width
                buf[h // kv_heads, c * 16 : c * 16 + 16, at : at + width] = y[16 * h : 16 * h + 16]
    me = lax.axis_index("tp")
    for d in range(tp):
        out_refs[d][...] = buf[lax.rem(me + d, tp)]


def scale_kernel(group, low_ref, q_ref, qs_ref, norm_ref):
    step = pl.program_id(0)
    tokens, heads, width = q_ref.shape
    qf = q_ref[...].astype(jnp.float32) * (LOG2E / math.sqrt(width))
    top = jnp.float32(0.0)
    for g in range(heads // group):
        x = qf[:, group * g : group * (g + 1)].reshape(tokens * group, width)
        qs_ref[g] = x.astype(jnp.bfloat16)
        top = jnp.maximum(top, top_norm(x))
    norm_ref[step] = top * 1.02


def assemble_kernel(tp, kv_heads, norm_ref, tag_ref, *refs):
    parts, o_ref, v_ref = refs[:tp], refs[tp], refs[tp + 1]
    part, width = parts[0].shape[0], v_ref.shape[1]
    rows = part * tp
    me = lax.axis_index("tp")
    for g in range(kv_heads):
        for d in range(tp):
            at = pl.multiple_of(lax.rem(me + tp - d, tp) * part, 16)
            o_ref[g, pl.ds(at, part)] = parts[d][:, 2 * width * g : 2 * width * g + width]
            v_ref[pl.ds(at, part)] = parts[d][:, 2 * width * g + width : 2 * width * (g + 1)].astype(jnp.float32)
        for j in range(rows // width):
            block = v_ref[j * width : (j + 1) * width].T
            o_ref[g, rows + j * width : rows + (j + 1) * width] = block.astype(jnp.bfloat16)
        o_ref[g, 2 * rows : 2 * rows + PAD] = tag_ref[...]
        top = top_norm(o_ref[g, :rows]) * 1.02
        o_ref[g, 2 * rows + PAD :] = jnp.full((PAD, width), top, jnp.float32).astype(jnp.bfloat16)


def fill_values(vt_ref, at, kv_ref, g, rows, count):
    width = kv_ref.shape[-1]
    more = vt_ref.shape[-2] - width
    for j in range(rows // width):
        cols = slice(j * width, (j + 1) * width)
        valid = j * width + lax.broadcasted_iota(jnp.int32, (1, width), 1) >= rows - count
        vt = kv_ref[g, rows + j * width : rows + (j + 1) * width].astype(jnp.float32)
        vt_ref[(*at, slice(0, width), cols)] = jnp.where(valid, vt, 0.0).astype(jnp.bfloat16)
        ones = jnp.ones((more, width), jnp.float32)
        vt_ref[(*at, slice(width, width + more), cols)] = jnp.where(valid, ones, 0.0).astype(jnp.bfloat16)


def general_tile(acc_ref, g, s, ok, vt):
    sums = vt.shape[0]
    old = acc_ref[g, sums : sums + 1]
    m = jnp.maximum(old, jnp.max(jnp.where(ok, s, NEG), axis=0, keepdims=True))
    p = jnp.where(ok, jnp.exp2(s - m), 0.0).astype(jnp.bfloat16)
    o = jnp.dot(vt, p, preferred_element_type=jnp.float32)
    acc_ref[g, :sums] = acc_ref[g, :sums] * jnp.exp2(old - m) + o
    acc_ref[g, sums:] = jnp.broadcast_to(m, (8, s.shape[1]))


def local_kernel(group, norm_ref, low_ref, qs_ref, own_ref, acc_ref, vt_ref):
    step = pl.program_id(1)
    width = own_ref.shape[2]
    rows = vt_ref.shape[1]
    sums = vt_ref.shape[0]
    lanes = TILE * group

    @pl.when(step == 0)
    def _():
        fill_values(vt_ref, (), own_ref, 0, rows, rows)

    kn = jnp.max(own_ref[0, 2 * rows + PAD :].astype(jnp.float32))
    fast = norm_ref[step] * kn <= SAFE * abs(SAFE)
    token = step * TILE + lax.broadcasted_iota(jnp.int32, (1, lanes), 1) // group
    low = low_ref[0:1]

    for i in range(rows // TILE):

        @pl.when(fast & (step == i))
        def _():
            keys = (i + 1) * TILE
            s = lax.dot_general(own_ref[0, :keys], qs_ref[0], NT, preferred_element_type=jnp.float32)
            at = lax.broadcasted_iota(jnp.int32, (keys, lanes), 0)
            p = jnp.where((at >= low) & (at <= token), jnp.exp2(s), 0.0).astype(jnp.bfloat16)
            acc_ref[0, :sums] = jnp.dot(vt_ref[:, :keys], p, preferred_element_type=jnp.float32)
            acc_ref[0, sums:] = jnp.zeros((8, lanes), jnp.float32)

    @pl.when(jnp.logical_not(fast))
    def _():
        acc_ref[0, :sums] = jnp.zeros((sums, lanes), jnp.float32)
        acc_ref[0, sums:] = jnp.full((8, lanes), NEG, jnp.float32)

        def tile(j, carry):
            at = pl.multiple_of(j * SMALL, SMALL)
            s = lax.dot_general(own_ref[0, pl.ds(at, SMALL)], qs_ref[0], NT, preferred_element_type=jnp.float32)
            pos = at + lax.broadcasted_iota(jnp.int32, (SMALL, lanes), 0)
            general_tile(acc_ref, 0, s, (pos >= low) & (pos <= token), vt_ref[:, pl.ds(at, SMALL)])
            return carry

        lax.fori_loop(0, ((step + 1) * TILE + SMALL - 1) // SMALL, tile, 0)


def far_kernel(group, last, norm_ref, tag_ref, qs_ref, acc_in_ref, *refs):
    blocks = 1 if last else 2
    if last:
        three_ref, two_flip_ref, o_ref, k_ref, vt_ref, acc_ref, n_ref, kn_ref = refs
        choices = (((two_flip_ref, True), (three_ref, False)),)
    else:
        flip_ref, two_ref, two_flip_ref, acc_ref, k_ref, vt_ref, n_ref, kn_ref = refs
        choices = (((flip_ref, True), (two_flip_ref, False)), ((two_ref, None),))
    step = pl.program_id(0)
    kv_heads, lanes, width = qs_ref.shape
    rows = vt_ref.shape[-1]
    sums = vt_ref.shape[-2]
    home = blocks * rows

    @pl.when(step == 0)
    def _():
        odd = lax.rem(lax.axis_index("cp"), 2) == 1
        own = tag_ref[...].astype(jnp.float32)
        at = lax.broadcasted_iota(jnp.int32, own.shape, 0) * width
        at = at + lax.broadcasted_iota(jnp.int32, own.shape, 1)
        first = jnp.max(jnp.where(at == 0, own, 0.0))
        count = lambda x: jnp.sum((x.astype(jnp.float32) == first).astype(jnp.float32)).astype(jnp.int32)
        n_ref[0] = count(own)
        kn_ref[0] = 0.0
        for b, choice in enumerate(choices):
            slot = blocks - 1 - b
            counts = [count(ref[0, 2 * rows : 2 * rows + PAD]) for ref, _ in choice]
            n_ref[1 + b] = counts[0] if len(counts) == 1 else jnp.where(odd, counts[0], counts[1])
            for ref, parity in choice:
                when = n_ref[1 + b] > 0
                if parity is not None:
                    when = when & (odd == parity)

                @pl.when(when)
                def _():
                    for g in range(kv_heads):
                        k_ref[g, slot * rows : (slot + 1) * rows] = ref[g, :rows]
                        fill_values(vt_ref, (g, slot), ref, g, rows, n_ref[1 + b])
                        kn_ref[0] = jnp.maximum(kn_ref[0], jnp.max(ref[g, 2 * rows + PAD :].astype(jnp.float32)))

    acc_ref[...] = acc_in_ref[...]
    reach = n_ref[0]
    back = n_ref[1] if last else n_ref[1] + n_ref[2]
    fast = norm_ref[step] * kn_ref[0] <= SAFE * abs(SAFE)
    for g in range(kv_heads):
        fast = fast & (jnp.max(jnp.abs(acc_in_ref[g, sums:])) == 0.0)
    token = step * TILE + lax.broadcasted_iota(jnp.int32, (1, lanes), 1) // group
    mine = token < reach
    some = (step * TILE < reach) & (back > 0)
    begin = (home - back) // SMALL * kv_heads

    def scores(g, at, keys):
        return lax.dot_general(k_ref[g, pl.ds(at, keys)], qs_ref[g], NT, preferred_element_type=jnp.float32)

    if last:

        @pl.when(fast & some)
        def _():
            def tile(j, carry):
                g = lax.rem(j, kv_heads)
                at = pl.multiple_of(j // kv_heads * SMALL, SMALL)
                p = jnp.exp2(scores(g, at, SMALL)).astype(jnp.bfloat16)
                o = jnp.dot(vt_ref[g, 0, :, pl.ds(at, SMALL)], p, preferred_element_type=jnp.float32)
                acc_ref[g, :sums] += jnp.where(mine, o, 0.0)
                return carry

            lax.fori_loop(begin, home // SMALL * kv_heads, tile, 0)

    else:

        @pl.when(fast & some)
        def _():
            first = jnp.where(back > rows, 0, 1)

            def block(j, carry):
                g = lax.rem(j, kv_heads)
                slot = first + j // kv_heads
                p = jnp.exp2(scores(g, pl.multiple_of(slot * rows, rows), rows)).astype(jnp.bfloat16)
                o = jnp.dot(vt_ref[g, slot], p, preferred_element_type=jnp.float32)
                acc_ref[g, :sums] += jnp.where(mine, o, 0.0)
                return carry

            lax.fori_loop(0, (blocks - first) * kv_heads, block, 0)

    @pl.when(jnp.logical_not(fast) & some)
    def _():
        def tile(j, carry):
            g = lax.rem(j, kv_heads)
            at = pl.multiple_of(j // kv_heads * SMALL, SMALL)
            s = scores(g, at, SMALL)
            pos = at + lax.broadcasted_iota(jnp.int32, (SMALL, lanes), 0)
            slot = at // rows
            vt = vt_ref[g, slot, :, pl.ds(pl.multiple_of(at - slot * rows, SMALL), SMALL)]
            general_tile(acc_ref, g, s, (pos >= home - back) & mine, vt)
            return carry

        lax.fori_loop(begin, home // SMALL * kv_heads, tile, 0)

    if last:
        outs = []
        for g in range(kv_heads):
            o = acc_ref[g, :width] * (1.0 / acc_ref[g, width : width + 1])
            outs.append(o.T.reshape(TILE, group, width))
        o_ref[...] = jnp.concatenate(outs, axis=1).astype(jnp.bfloat16)


def shards(queries, key_states, value_states, doc_ids):
    rows, q_heads, width = queries.shape
    tp = lax.axis_size("tp")
    cp = lax.axis_size("cp")
    part, heads = key_states.shape[:2]
    kv_heads = heads // tp
    group = q_heads // kv_heads
    lanes = TILE * group
    steps = rows // TILE
    params = pltpu.CompilerParams(vmem_limit_bytes=VMEM_LIMIT)
    vmem = pl.BlockSpec(memory_space=pltpu.VMEM)
    smem = pl.BlockSpec(memory_space=pltpu.SMEM)

    tag = (doc_ids + 1).astype(jnp.bfloat16).reshape(rows // width, width)
    tag = jnp.pad(tag, ((0, PAD - tag.shape[0]), (0, 0)))
    low = jnp.sum((doc_ids[None, :] < doc_ids[:, None]).astype(jnp.int32), axis=1)
    low = jnp.broadcast_to(jnp.repeat(low, group)[None], (8, rows * group))

    pieces = pl.pallas_call(
        functools.partial(pack_kernel, tp, kv_heads),
        in_specs=[vmem, vmem],
        out_specs=[vmem] * tp,
        out_shape=[jax.ShapeDtypeStruct((part, 2 * kv_heads * width), jnp.bfloat16)] * tp,
        scratch_shapes=[pltpu.VMEM((tp, part, 2 * kv_heads * width), jnp.bfloat16)],
        compiler_params=params,
        name="pack",
    )(key_states.reshape(part * heads, width), value_states.reshape(part * heads, width))
    mine = [pieces[0]]
    for d in range(1, tp):
        mine.append(lax.ppermute(pieces[d], "tp", [(i, (i + d) % tp) for i in range(tp)]))

    qs, norms = pl.pallas_call(
        functools.partial(scale_kernel, group),
        grid=(steps,),
        in_specs=[pl.BlockSpec(memory_space=pl.ANY), pl.BlockSpec((TILE, q_heads, width), lambda i: (i, 0, 0))],
        out_specs=[pl.BlockSpec((kv_heads, lanes, width), lambda i: (0, i, 0)), smem],
        out_shape=[
            jax.ShapeDtypeStruct((kv_heads, rows * group, width), jnp.bfloat16),
            jax.ShapeDtypeStruct((steps,), jnp.float32),
        ],
        compiler_params=params,
        name="scale",
    )(low, queries)
    size = (kv_heads, 2 * rows + 2 * PAD, width)
    own = pl.pallas_call(
        functools.partial(assemble_kernel, tp, kv_heads),
        in_specs=[smem] + [vmem] * (tp + 1),
        out_specs=vmem,
        out_shape=jax.ShapeDtypeStruct(size, jnp.bfloat16),
        scratch_shapes=[pltpu.VMEM((rows, width), jnp.float32)],
        compiler_params=params,
        name="assemble",
    )(norms, tag, *mine)

    flip_route = [(i, i ^ 1) for i in range(cp)]
    two = lax.ppermute(own, "cp", [(i, i + 2) for i in range(cp - 2)])
    flip = lax.ppermute(own, "cp", flip_route)

    sums = width + 16
    acc = pl.pallas_call(
        functools.partial(local_kernel, group),
        grid=(kv_heads, steps),
        in_specs=[
            smem,
            pl.BlockSpec((8, lanes), lambda g, i: (0, i)),
            pl.BlockSpec((1, lanes, width), lambda g, i: (g, i, 0)),
            pl.BlockSpec((1, *size[1:]), lambda g, i: (g, 0, 0)),
        ],
        out_specs=pl.BlockSpec((1, sums + 8, lanes), lambda g, i: (g, 0, i)),
        out_shape=jax.ShapeDtypeStruct((kv_heads, sums + 8, rows * group), jnp.float32),
        scratch_shapes=[pltpu.VMEM((sums, rows), jnp.bfloat16)],
        compiler_params=params,
        cost_estimate=pl.CostEstimate(flops=8 * 10**9, bytes_accessed=10**7, transcendentals=0),
        name="local",
    )(norms, low, qs, own)
    late, acc = lax.optimization_barrier((own, acc))
    three = lax.ppermute(late, "cp", [(i, i + 3) for i in range(1, cp - 3, 2)])
    two, acc = lax.optimization_barrier((two, acc))
    two_flip = lax.ppermute(two, "cp", flip_route)
    whole = pl.BlockSpec(size, lambda i: (0, 0, 0))
    acc_spec = pl.BlockSpec((kv_heads, sums + 8, lanes), lambda i: (0, 0, i))
    in_specs = [smem, vmem, pl.BlockSpec((kv_heads, lanes, width), lambda i: (0, i, 0)), acc_spec]
    slots = lambda blocks: [
        pltpu.VMEM((kv_heads, blocks * rows, width), jnp.bfloat16),
        pltpu.VMEM((kv_heads, blocks, sums, rows), jnp.bfloat16),
    ]
    scalars = [pltpu.SMEM((WIN,), jnp.int32), pltpu.SMEM((1,), jnp.float32)]
    acc = pl.pallas_call(
        functools.partial(far_kernel, group, False),
        grid=(steps,),
        in_specs=in_specs + [whole] * 3,
        out_specs=acc_spec,
        out_shape=jax.ShapeDtypeStruct(acc.shape, jnp.float32),
        scratch_shapes=[*slots(2), *scalars],
        compiler_params=params,
        cost_estimate=pl.CostEstimate(flops=2 * 10**10, bytes_accessed=10**7, transcendentals=0),
        name="near",
    )(norms, tag, qs, acc, flip, two, two_flip)
    return pl.pallas_call(
        functools.partial(far_kernel, group, True),
        grid=(steps,),
        in_specs=in_specs + [whole] * 2,
        out_specs=pl.BlockSpec((TILE, q_heads, width), lambda i: (i, 0, 0)),
        out_shape=jax.ShapeDtypeStruct(queries.shape, jnp.bfloat16),
        scratch_shapes=[*slots(1), pltpu.VMEM((kv_heads, sums + 8, lanes), jnp.float32), *scalars],
        compiler_params=params,
        name="last",
    )(norms, tag, qs, acc, three, two_flip)


def solution(mesh):
    in_specs = (
        P("cp", "tp", None),
        P(("cp", "tp"), None, None),
        P(("cp", "tp"), None, None),
        P("cp"),
    )
    out_specs = P("cp", "tp", None)
    return jax.shard_map(shards, mesh=mesh, in_specs=in_specs, out_specs=out_specs, check_vma=False)
```
